32 devices in a mesh: fsdp: 2 (over x), ctx: 4 (over y, core), tp: 4 (over z).
Axes of the slice: x: 2, y: 2, z: 4, core: 2. Of those that a mesh axis runs over, the one named last changes fastest.
Arguments:
- tokens: bfloat16 [12288, 768], P(('fsdp', 'ctx')), may hold values from -6 to 6
- cotangent: bfloat16 [12288, 768], P(('fsdp', 'ctx')), may hold values from -6 to 6
- doc_lengths: int32 [2, 3], P('fsdp'), may hold values from 1 to 5376, 6144 in all within a row
- ln1_gain: bfloat16 [768], P('fsdp'), may hold values from 0.099609375 to 1.8984375
- ln1_bias: bfloat16 [768], P('fsdp'), may hold values from -4 to 4
- ln2_gain: bfloat16 [768], P('fsdp'), may hold values from 0.099609375 to 1.8984375
- ln2_bias: bfloat16 [768], P('fsdp'), may hold values from -4 to 4
- w_qkv: bfloat16 [3, 768, 768], P(None, 'fsdp', 'tp'), may hold values from -0.21875 to 0.21875
- qv_bias: bfloat16 [2, 768], P(None, ('tp', 'fsdp')), may hold values from -6 to 6
- w_out: bfloat16 [768, 768], P('tp', 'fsdp'), may hold values from -1.75 to 1.75
- out_bias: bfloat16 [768], P('fsdp'), may hold values from -4 to 4
- w_in: bfloat16 [768, 3072], P('fsdp', 'tp'), may hold values from -0.21875 to 0.21875
- in_bias: bfloat16 [3072], P(('tp', 'fsdp')), may hold values from -6 to 6
- w_back: bfloat16 [3072, 768], P('tp', 'fsdp'), may hold values from -0.109375 to 0.109375
- back_bias: bfloat16 [768], P('fsdp'), may hold values from -4 to 4
Outputs:
- mixed: bfloat16 [12288, 768], P(('fsdp', 'ctx'))
- input_grad: float32 [12288, 768], P(('fsdp', 'ctx'))
- ln1_gain_grad: float32 [768], P('fsdp')
- ln1_bias_grad: float32 [768], P('fsdp')
- ln2_gain_grad: float32 [768], P('fsdp')
- ln2_bias_grad: float32 [768], P('fsdp')
- w_qkv_grad: float32 [3, 768, 768], P(None, 'fsdp', 'tp')
- qv_bias_grad: float32 [2, 768], P(None, ('tp', 'fsdp'))
- w_out_grad: float32 [768, 768], P('tp', 'fsdp')
- out_bias_grad: float32 [768], P('fsdp')
- w_in_grad: float32 [768, 3072], P('fsdp', 'tp')
- in_bias_grad: float32 [3072], P(('tp', 'fsdp'))
- w_back_grad: float32 [3072, 768], P('tp', 'fsdp')
- back_bias_grad: float32 [768], P('fsdp')
The draws below stay inside these ranges and needn't reach their ends.
Inputs may be any that keep to these rules, and one draw needn't show every extreme that they name: `doc_lengths`: row g lists the lengths of the documents packed in order into group g's 6144 tokens; each row sums to 6144 and its largest entry is 5376.
All inputs are finite; a program needn't handle non-finite values.
Results may differ from the reference program's by a relative error of at most 0.023.
Values may be sent and summed in bfloat16 or wider, within the bound.
A program may use at most 128 MiB of HBM per device.

```python
import math
import jax
import jax.numpy as jnp
import numpy as np
from jax import lax

D = 768
HEADS = 12
HEAD = 64
FF = 3072
NSEQ = 3
PACK = 6144
LONGEST = 5376
TOKENS = 12288
N_FSDP = 2


def level_of(own_key, shape, split, low, high):
    level = 1.0
    for axis_at, blocks in split:
        heights = jax.random.uniform(jax.random.fold_in(jax.random.fold_in(own_key, 6), axis_at), (blocks,), jnp.float32, low / len(split), high / len(split))
        level = level * jnp.repeat(jnp.exp(heights), shape[axis_at] // blocks).reshape((-1,) + (1,) * (len(shape) - 1 - axis_at))
    return level


def split_up(number_of, total, limit, lean):
    portions = [(1 << 20) // math.isqrt(grade ** lean) + 1 for grade in range(2, number_of + 1)]
    surplus, counts = total - limit - (number_of - 1), [1] * (number_of - 1)
    while surplus > 0:
        free = [i for i in range(number_of - 1) if counts[i] < limit]
        whole, left = sum([portions[i] for i in free]), surplus
        for i in free:
            extra = min(limit - counts[i], max(1, left * portions[i] // whole), surplus)
            counts[i] = counts[i] + extra
            surplus = surplus - extra
    return np.array([limit] + counts)


def ragged_sizes(own_key, count, total, most, slope):
    if count == 2:
        one = jax.random.randint(own_key, (), max(1, total - most), min(most, total - 1) + 1)
        return jnp.stack([one, total - one])
    sizes = jnp.asarray(split_up(count, total, most, slope), jnp.int32)
    pairs = (count - 1) // 2
    source_of, receiver = sizes[1:1 + 2 * pairs:2], sizes[2:2 + 2 * pairs:2]
    room = jnp.minimum(source_of - 1, most - receiver)
    moved = jax.random.randint(jax.random.fold_in(own_key, 1), (pairs,), 0, 1 << 20) % (room + 1)
    sizes = sizes.at[1:1 + 2 * pairs:2].set(source_of - moved).at[2:2 + 2 * pairs:2].set(receiver + moved)
    return sizes[jax.random.permutation(jax.random.fold_in(own_key, 2), count)]


def bell_draw(rng, dims, scale, limit, pieces=(), held_as=jnp.bfloat16):
    values = jax.random.normal(rng, dims, jnp.float32) * scale
    if len(pieces) > 0:
        values = level_of(rng, dims, pieces, -0.22, 0.18) * values
    return jnp.clip(values, min=-limit, max=limit).astype(held_as)


def setup_inputs(seed: int = 0) -> dict:
    streams_of = jax.random.split(jax.random.key(seed), 16)
    tokens = bell_draw(streams_of[0], (TOKENS, D), 1.0, 6.0, ((0, 8),))
    cotangent = bell_draw(streams_of[1], (TOKENS, D), 1.0, 6.0, ((0, 8),))
    doc_lengths = jax.vmap(lambda own: ragged_sizes(own, NSEQ, PACK, LONGEST, 2))(jax.random.split(streams_of[2], N_FSDP)).reshape((N_FSDP, NSEQ)).astype(jnp.int32)
    ln1_gain = jnp.clip(1.0 + 0.18 * jax.random.normal(streams_of[3], (D,), jnp.float32), 0.099609375, 1.8984375).astype(jnp.bfloat16)
    ln1_bias = bell_draw(streams_of[4], (D,), 0.3, 4.0, ((0, 2),))
    ln2_gain = jnp.clip(1.0 + 0.18 * jax.random.normal(streams_of[5], (D,), jnp.float32), 0.099609375, 1.8984375).astype(jnp.bfloat16)
    ln2_bias = bell_draw(streams_of[6], (D,), 0.3, 4.0, ((0, 2),))
    w_qkv = bell_draw(streams_of[7], (3, D, D), D ** -0.5, 0.21875, ((1, 2), (2, 4)))
    qv_bias = bell_draw(streams_of[8], (2, D), 0.5, 6.0, ((1, 8),))
    w_out = bell_draw(streams_of[9], (D, D), (max(D // 64, 1)) ** -0.5, 1.75, ((0, 4), (1, 2)))
    out_bias = bell_draw(streams_of[10], (D,), 0.3, 4.0, ((0, 2),))
    w_in = bell_draw(streams_of[11], (D, FF), D ** -0.5, 0.21875, ((0, 2), (1, 4)))
    in_bias = bell_draw(streams_of[12], (FF,), 0.5, 6.0, ((0, 8),))
    w_back = bell_draw(streams_of[13], (FF, D), FF ** -0.5, 0.109375, ((0, 4), (1, 2)))
    back_bias = bell_draw(streams_of[14], (D,), 0.3, 4.0, ((0, 2),))
    return dict(tokens=tokens, cotangent=cotangent, doc_lengths=doc_lengths, ln1_gain=ln1_gain, ln1_bias=ln1_bias, ln2_gain=ln2_gain, ln2_bias=ln2_bias, w_qkv=w_qkv, qv_bias=qv_bias, w_out=w_out, out_bias=out_bias, w_in=w_in, in_bias=in_bias, w_back=w_back, back_bias=back_bias)


@jax.custom_vjp
def low(v):
    return lax.optimization_barrier(v.astype(jnp.bfloat16)).astype(jnp.float32)

@jax.custom_vjp
def low_back(v):
    return v

def low_keep(v):
    return (low(v), None)

def low_pass(kept, grad):
    return (grad,)

def back_keep(v):
    return (v, None)

def back_low(kept, grad):
    return (low(grad),)
low.defvjp(low_keep, low_pass)
low_back.defvjp(back_keep, back_low)
norm_epsilon = 1e-05
masked_score = -1e+30

def layer_norm(inputs_f, norm_gain, norm_shift):
    centred = inputs_f - lax.optimization_barrier(jnp.mean(inputs_f, axis=-1, keepdims=True))
    spread = lax.optimization_barrier(jnp.mean(centred * centred, axis=-1, keepdims=True))
    return centred * lax.rsqrt(spread + norm_epsilon) * norm_gain + norm_shift

def product(left_side, right_side):
    return jnp.dot(left_side, right_side, precision=lax.Precision.HIGHEST)

def rounded_both(matrix):
    return low_back(low(matrix))

def heads_first(matrix):
    return matrix.reshape(PACK, HEADS, HEAD).transpose(1, 0, 2)

def group_layer(tokens_f, lengths, params):
    gain_one, shift_one, gain_two, shift_two, qkv_weight, qv_shift, out_weight, out_shift, in_weight, in_shift, back_weight, back_shift = params
    normed_one = low(layer_norm(tokens_f, gain_one, shift_one))
    queries = rounded_both(product(normed_one, qkv_weight[0]) + qv_shift[0])
    key_rows = rounded_both(product(normed_one, qkv_weight[1]))
    value_rows = rounded_both(product(normed_one, qkv_weight[2]) + qv_shift[1])
    places = jnp.arange(PACK, dtype=jnp.int32)
    bounds = jnp.cumsum(lengths)[:-1]
    document = lax.optimization_barrier(jnp.sum((places[:, None] >= bounds[None, :]).astype(jnp.int32), axis=1))
    allowed = (document[:, None] == document[None, :]) & (places[None, :] <= places[:, None])
    score_scale = HEAD ** (-0.5)

    def one_head(head_parts):
        head_queries, head_keys, head_values = head_parts
        scores = low_back(product(head_queries, head_keys.T) * score_scale)
        scores = jnp.where(allowed, scores, masked_score)
        shifted = jnp.exp(scores - lax.optimization_barrier(jnp.max(scores, axis=-1, keepdims=True)))
        attention = shifted / lax.optimization_barrier(jnp.sum(shifted, axis=-1, keepdims=True))
        return product(low(attention), head_values)
    attended = lax.map(jax.checkpoint(one_head), (heads_first(queries), heads_first(key_rows), heads_first(value_rows)))
    attended = rounded_both(attended.transpose(1, 0, 2).reshape(PACK, D))
    residual = tokens_f + low_back(product(attended, out_weight) + out_shift)
    normed_two = low(layer_norm(residual, gain_two, shift_two))
    hidden = low_back(product(normed_two, in_weight) + in_shift)
    active = low(jax.nn.gelu(hidden, approximate=True))
    return residual + low_back(product(active, back_weight) + back_shift)

def reference(tokens, cotangent, doc_lengths, ln1_gain, ln1_bias, ln2_gain, ln2_bias, w_qkv, qv_bias, w_out, out_bias, w_in, in_bias, w_back, back_bias):
    params = tuple((argument.astype(jnp.float32) for argument in (ln1_gain, ln1_bias, ln2_gain, ln2_bias, w_qkv, qv_bias, w_out, out_bias, w_in, in_bias, w_back, back_bias)))
    groups = tokens.astype(jnp.float32).reshape(N_FSDP, PACK, D)
    cot_groups = cotangent.astype(jnp.float32).reshape(N_FSDP, PACK, D)

    def group_step(totals, group_piece):
        group_tokens, group_cot, lengths = group_piece

        def forward(tokens_f, weights):
            return group_layer(tokens_f, lengths, weights)
        result, pull_back = jax.vjp(forward, group_tokens, params)
        token_grad, weight_grads = pull_back(group_cot)
        return (jax.tree.map(jnp.add, totals, weight_grads), (result, token_grad))
    zero_grads = jax.tree.map(jnp.zeros_like, params)
    weight_totals, (results, token_grads) = lax.scan(group_step, zero_grads, (groups, cot_groups, doc_lengths))
    return (results.reshape(TOKENS, D).astype(jnp.bfloat16), token_grads.reshape(TOKENS, D), weight_totals[0], weight_totals[1], weight_totals[2], weight_totals[3], weight_totals[4], weight_totals[5], weight_totals[6], weight_totals[7], weight_totals[8], weight_totals[9], weight_totals[10], weight_totals[11])
```

```python
import jax
import jax.numpy as jnp
from jax import lax
from jax.experimental import pallas as pl
from jax.experimental.pallas import tpu as pltpu
from jax.sharding import PartitionSpec as P

HEAD = 64


norm_epsilon = 1e-05
masked_score = -1e30


def layer_norm(inputs_f, norm_gain, norm_shift):
    centred = inputs_f - jnp.mean(inputs_f, axis=-1, keepdims=True)
    spread = jnp.mean(centred * centred, axis=-1, keepdims=True)
    return centred * lax.rsqrt(spread + norm_epsilon) * norm_gain + norm_shift


def smooth_act(inputs_f):
    return jax.nn.gelu(inputs_f, approximate=True)


def mat_product(left_side, right_side):
    return jnp.dot(left_side, right_side, preferred_element_type=jnp.float32)


def left_product(left_side, right_side):
    return lax.dot_general(
        left_side, right_side, (((0,), (0,)), ((), ())), preferred_element_type=jnp.float32
    )


def right_product(left_side, right_side):
    return lax.dot_general(
        left_side, right_side, (((1,), (1,)), ((), ())), preferred_element_type=jnp.float32
    )


def column_sums(matrix):
    return jnp.sum(matrix.astype(jnp.float32), axis=0)


LANES = 128
Q_BLOCK = 256
K_BLOCK = 512
VMEM_BYTES = 60 * 1024 * 1024


def doc_start(place, bound_one, bound_two):
    return jnp.where(place >= bound_two, bound_two, jnp.where(place >= bound_one, bound_one, 0))


def widen(piece, tail):
    return jnp.concatenate([piece, tail], axis=1)


def lay_out_heads(kv_ref, key_s, value_s):
    heads, rows_all, _ = key_s.shape
    width = heads * HEAD
    lane = lax.broadcasted_iota(jnp.int32, (K_BLOCK, LANES - HEAD), 1)
    ones = jnp.where(lane < 3, 1.0, 0.0).astype(jnp.bfloat16)

    def step(block, carry):
        rows = pl.ds(pl.multiple_of(block * K_BLOCK, K_BLOCK), K_BLOCK)
        slab = kv_ref[rows, :]
        for h in range(heads):
            key_s[h, rows, :] = widen(slab[:, h * HEAD : (h + 1) * HEAD], ones)
            value_s[h, rows, :] = widen(slab[:, width + h * HEAD : width + (h + 1) * HEAD], ones)
        return carry

    lax.fori_loop(0, rows_all // K_BLOCK, step, 0)


def block_ranges(first, place_ref):
    bound_one, bound_two = place_ref[0], place_ref[1]
    last = first + Q_BLOCK - 1
    begin = doc_start(first, bound_one, bound_two) // K_BLOCK
    end = last // K_BLOCK + 1
    clear_from = (doc_start(last, bound_one, bound_two) + K_BLOCK - 1) // K_BLOCK
    clear_from = jnp.minimum(jnp.maximum(clear_from, begin), end)
    clear_to = jnp.minimum(jnp.maximum((first + 1) // K_BLOCK, clear_from), end)
    return begin, clear_from, clear_to, end


def three_loops(ranges, visit, carry):
    begin, clear_from, clear_to, end = ranges
    carry = lax.fori_loop(begin, clear_from, lambda i, c: visit(i, c, True), carry)
    carry = lax.fori_loop(clear_from, clear_to, lambda i, c: visit(i, c, False), carry)
    return lax.fori_loop(clear_to, end, lambda i, c: visit(i, c, True), carry)


def attend_kernel(place_ref, q_ref, kv_ref, out_ref, qa_ref, key_s, value_s, acc_s):
    heads = key_s.shape[0]
    lay_out_heads(kv_ref, key_s, value_s)
    half = q_ref.shape[0] // 2
    bound_one, bound_two = place_ref[0], place_ref[1]
    lane = lax.broadcasted_iota(jnp.int32, (Q_BLOCK, LANES), 1)
    zeros = jnp.zeros((Q_BLOCK, LANES - HEAD), jnp.float32)

    for part in range(2):

        def q_step(block, carry0, part=part):
            first = place_ref[2 + part] + block * Q_BLOCK
            rows = pl.ds(pl.multiple_of(part * half + block * Q_BLOCK, Q_BLOCK), Q_BLOCK)
            q_all = q_ref[rows, :].astype(jnp.float32) * (HEAD**-0.5)
            q_wide = [widen(q_all[:, h * HEAD : (h + 1) * HEAD], zeros) for h in range(heads)]
            q_low = [q.astype(jnp.bfloat16) for q in q_wide]
            acc_s[...] = jnp.zeros_like(acc_s)
            q_place = first + lax.broadcasted_iota(jnp.int32, (Q_BLOCK, 1), 0)
            q_start = doc_start(q_place, bound_one, bound_two)

            def visit(kb, maxima, masked):
                keys = pl.ds(pl.multiple_of(kb * K_BLOCK, K_BLOCK), K_BLOCK)
                if masked:
                    k_place = kb * K_BLOCK + lax.broadcasted_iota(
                        jnp.int32, (Q_BLOCK, K_BLOCK), 1
                    )
                    allowed = (k_place <= q_place) & (k_place >= q_start)
                new_maxima = []
                for h in range(heads):
                    scores = right_product(q_low[h], key_s[h, keys, :])
                    if masked:
                        scores = jnp.where(allowed, scores, masked_score)
                    new_max = jnp.maximum(maxima[h], jnp.max(scores, axis=1, keepdims=True))
                    prob = jnp.exp(scores - new_max).astype(jnp.bfloat16)
                    acc_s[h] = acc_s[h] * jnp.exp(maxima[h] - new_max) + mat_product(
                        prob, value_s[h, keys, :]
                    )
                    new_maxima.append(new_max)
                return tuple(new_maxima)

            start = tuple(jnp.full((Q_BLOCK, 1), masked_score, jnp.float32) for _ in range(heads))
            maxima = three_loops(block_ranges(first, place_ref), visit, start)
            outs = []
            for h in range(heads):
                total = acc_s[h]
                row_sum = total[:, HEAD : HEAD + 1]
                outs.append(total[:, :HEAD] / row_sum)
                minus = -(maxima[h] + jnp.log(row_sum))
                high = minus.astype(jnp.bfloat16).astype(jnp.float32)
                middle = (minus - high).astype(jnp.bfloat16).astype(jnp.float32)
                wide = jnp.where(lane == HEAD, high, q_wide[h])
                wide = jnp.where(lane == HEAD + 1, middle, wide)
                wide = jnp.where(lane == HEAD + 2, minus - high - middle, wide)
                qa_ref[h, rows, :] = wide.astype(jnp.bfloat16)
            out_ref[rows, :] = jnp.concatenate(outs, axis=1)
            return carry0

        lax.fori_loop(0, half // Q_BLOCK, q_step, 0)


def attend_back_kernel(
    place_ref, qa_ref, go_ref, out_ref, kv_ref, dq_ref, dkv_ref, key_s, value_s, dk_s, dv_s, dq_s
):
    heads, rows_all, _ = key_s.shape
    lay_out_heads(kv_ref, key_s, value_s)
    dk_s[...] = jnp.zeros_like(dk_s)
    dv_s[...] = jnp.zeros_like(dv_s)
    half = go_ref.shape[0] // 2
    bound_one, bound_two = place_ref[0], place_ref[1]
    lane = lax.broadcasted_iota(jnp.int32, (Q_BLOCK, LANES), 1)
    zeros = jnp.zeros((Q_BLOCK, LANES - HEAD), jnp.float32)

    for part in range(2):

        def q_step(block, carry0, part=part):
            first = place_ref[2 + part] + block * Q_BLOCK
            rows = pl.ds(pl.multiple_of(part * half + block * Q_BLOCK, Q_BLOCK), Q_BLOCK)
            go_all = go_ref[rows, :].astype(jnp.float32)
            weighted = go_all * out_ref[rows, :]
            go_low, q_low = [], []
            for h in range(heads):
                cols = slice(h * HEAD, (h + 1) * HEAD)
                minus = -jnp.sum(weighted[:, cols], axis=1, keepdims=True)
                high = minus.astype(jnp.bfloat16).astype(jnp.float32)
                wide = widen(go_all[:, cols], zeros)
                wide = jnp.where(lane == HEAD, high, wide)
                wide = jnp.where(lane == HEAD + 1, minus - high, wide)
                go_low.append(wide.astype(jnp.bfloat16))
                q_low.append(qa_ref[h, rows, :])
            dq_s[...] = jnp.zeros_like(dq_s)
            q_place = first + lax.broadcasted_iota(jnp.int32, (1, Q_BLOCK), 1)
            q_start = doc_start(q_place, bound_one, bound_two)

            def visit(kb, carry, masked):
                keys = pl.ds(pl.multiple_of(kb * K_BLOCK, K_BLOCK), K_BLOCK)
                if masked:
                    k_place = kb * K_BLOCK + lax.broadcasted_iota(
                        jnp.int32, (K_BLOCK, Q_BLOCK), 0
                    )
                    allowed = (k_place <= q_place) & (k_place >= q_start)
                for h in range(heads):
                    key_block = key_s[h, keys, :]
                    scores = right_product(key_block, q_low[h])
                    if masked:
                        scores = jnp.where(allowed, scores, masked_score)
                    prob = jnp.exp(scores)
                    grad_prob = right_product(value_s[h, keys, :], go_low[h])
                    grad_scores = (prob * grad_prob).astype(jnp.bfloat16)
                    dv_s[h, keys, :] += mat_product(prob.astype(jnp.bfloat16), go_low[h])
                    dk_s[h, keys, :] += mat_product(grad_scores, q_low[h])
                    dq_s[h] += left_product(grad_scores, key_block)
                return carry

            three_loops(block_ranges(first, place_ref), visit, 0)
            dq_ref[rows, :] = jnp.concatenate(
                [dq_s[h][:, :HEAD] * (HEAD**-0.5) for h in range(heads)], axis=1
            ).astype(jnp.bfloat16)
            return carry0

        lax.fori_loop(0, half // Q_BLOCK, q_step, 0)

    def store(block, carry):
        rows = pl.ds(pl.multiple_of(block * K_BLOCK, K_BLOCK), K_BLOCK)
        dkv_ref[rows, :] = jnp.concatenate(
            [dk_s[h, rows, :][:, :HEAD] for h in range(heads)]
            + [dv_s[h, rows, :][:, :HEAD] for h in range(heads)],
            axis=1,
        ).astype(jnp.bfloat16)
        return carry

    lax.fori_loop(0, rows_all // K_BLOCK, store, 0)


def in_vmem(count):
    return [pl.BlockSpec(memory_space=pltpu.VMEM)] * count


def attend(place, queries, kv_all):
    rows, width = queries.shape
    rows_all = kv_all.shape[0]
    heads = width // HEAD
    pairs = rows * rows_all * heads // 2
    return pl.pallas_call(
        attend_kernel,
        out_shape=(
            jax.ShapeDtypeStruct((rows, width), jnp.float32),
            jax.ShapeDtypeStruct((heads, rows, LANES), jnp.bfloat16),
        ),
        in_specs=[pl.BlockSpec(memory_space=pltpu.SMEM)] + in_vmem(2),
        out_specs=tuple(in_vmem(2)),
        scratch_shapes=[
            pltpu.VMEM((heads, rows_all, LANES), jnp.bfloat16),
            pltpu.VMEM((heads, rows_all, LANES), jnp.bfloat16),
            pltpu.VMEM((heads, Q_BLOCK, LANES), jnp.float32),
        ],
        compiler_params=pltpu.CompilerParams(vmem_limit_bytes=VMEM_BYTES),
        cost_estimate=pl.CostEstimate(
            flops=pairs * 4 * 4 * HEAD, bytes_accessed=8 << 20, transcendentals=pairs
        ),
    )(place, queries, kv_all)


def attend_back(place, queries_wide, grad_out, attn_out, kv_all):
    rows, width = grad_out.shape
    rows_all = kv_all.shape[0]
    heads = width // HEAD
    pairs = rows * rows_all * heads // 2
    return pl.pallas_call(
        attend_back_kernel,
        out_shape=(
            jax.ShapeDtypeStruct((rows, width), jnp.bfloat16),
            jax.ShapeDtypeStruct((rows_all, 2 * width), jnp.bfloat16),
        ),
        in_specs=[pl.BlockSpec(memory_space=pltpu.SMEM)] + in_vmem(4),
        out_specs=tuple(in_vmem(2)),
        scratch_shapes=[
            pltpu.VMEM((heads, rows_all, LANES), jnp.bfloat16),
            pltpu.VMEM((heads, rows_all, LANES), jnp.bfloat16),
            pltpu.VMEM((heads, rows_all, LANES), jnp.float32),
            pltpu.VMEM((heads, rows_all, LANES), jnp.float32),
            pltpu.VMEM((heads, Q_BLOCK, LANES), jnp.float32),
        ],
        compiler_params=pltpu.CompilerParams(vmem_limit_bytes=VMEM_BYTES),
        cost_estimate=pl.CostEstimate(
            flops=pairs * 10 * 4 * HEAD, bytes_accessed=12 << 20, transcendentals=pairs
        ),
    )(place, queries_wide, grad_out, attn_out, kv_all)


def swap_halves(rows):
    size = lax.axis_size("ctx")
    half = rows.shape[0] // 2
    moved = lax.ppermute(rows[half:], "ctx", [(i, size - 1 - i) for i in range(size)])
    return jnp.concatenate([rows[:half], moved], axis=0)


def partner(value, distance):
    size = lax.axis_size("ctx")
    return lax.ppermute(value, "ctx", [(i, i ^ distance) for i in range(size)])


def halve(block, distance):
    bit = (lax.axis_index("ctx") // distance) % 2
    split = block.reshape(block.shape[:-2] + (2, block.shape[-2] // 2, block.shape[-1]))
    axis = split.ndim - 3
    keep = lax.dynamic_index_in_dim(split, bit, axis, keepdims=False)
    send = lax.dynamic_index_in_dim(split, 1 - bit, axis, keepdims=False)
    got = partner(send, distance)
    return (keep.astype(jnp.float32) + got.astype(jnp.float32)).astype(jnp.bfloat16)


def unhalve(block, distance):
    bit = (lax.axis_index("ctx") // distance) % 2
    other = partner(block, distance)
    low = jnp.where(bit == 0, block, other)
    high = jnp.where(bit == 0, other, block)
    return jnp.concatenate([low, high], axis=-2)


def reduce_shards(block):
    size = lax.axis_size("ctx")
    distances = [1 << i for i in range(size.bit_length() - 1)]
    block = halve(block, 1)
    if block.shape[0] == 2:
        bit = lax.axis_index("fsdp")
        keep = lax.dynamic_index_in_dim(block, bit, 0, keepdims=False)
        send = lax.dynamic_index_in_dim(block, 1 - bit, 0, keepdims=False)
        got = lax.ppermute(send, "fsdp", [(0, 1), (1, 0)])
        block = (keep.astype(jnp.float32) + got.astype(jnp.float32)).astype(jnp.bfloat16)
    else:
        block = lax.psum_scatter(block, "fsdp", scatter_dimension=0, tiled=False)
    for distance in distances[1:]:
        block = halve(block, distance)
    for distance in distances[::-1]:
        block = unhalve(block, distance)
    return block


def on_device(
    tokens,
    cotangent,
    doc_lengths,
    ln1_gain,
    ln1_bias,
    ln2_gain,
    ln2_bias,
    w_qkv,
    qv_bias,
    w_out,
    out_bias,
    w_in,
    in_bias,
    w_back,
    back_bias,
):
    rows_here = tokens.shape[0]
    ctx_size = lax.axis_size("ctx")
    ctx_place = lax.axis_index("ctx")
    fsdp = lax.axis_size("fsdp")
    model = tokens.shape[1]
    part_d = model // fsdp
    qkv_full = lax.all_gather(w_qkv, "fsdp", axis=1, tiled=True)
    vectors = jnp.concatenate(
        [
            ln1_gain,
            ln1_bias,
            ln2_gain,
            ln2_bias,
            out_bias,
            back_bias,
            qv_bias[0],
            qv_bias[1],
            in_bias,
        ]
    )
    vectors = lax.all_gather(vectors, "fsdp", axis=0).astype(jnp.float32)
    sizes = [part_d] * 6 + [qv_bias.shape[1]] * 2 + [in_bias.shape[0]]
    pieces, offset = [], 0
    for size in sizes:
        pieces.append(vectors[:, offset : offset + size].reshape(fsdp * size))
        offset += size
    gain_one, shift_one, gain_two, shift_two, out_shift, back_shift, q_shift, v_shift, in_shift = (
        pieces
    )
    out_full = lax.all_gather(w_out, "fsdp", axis=1, tiled=True)
    in_full = lax.all_gather(w_in, "fsdp", axis=0, tiled=True)
    back_full = lax.all_gather(w_back, "fsdp", axis=1, tiled=True)
    local_width = qkv_full.shape[2]
    tokens_f = tokens.astype(jnp.float32)
    cot_f = cotangent.astype(jnp.float32)
    normed_one = layer_norm(tokens_f, gain_one, shift_one).astype(jnp.bfloat16)
    key_rows = mat_product(normed_one, qkv_full[1]).astype(jnp.bfloat16)
    value_rows = (mat_product(normed_one, qkv_full[2]) + v_shift).astype(jnp.bfloat16)
    kv_all = lax.all_gather(
        jnp.concatenate([key_rows, value_rows], axis=1), "ctx", axis=0, tiled=True
    )
    queries = (mat_product(normed_one, qkv_full[0]) + q_shift).astype(jnp.bfloat16)
    queries = swap_halves(queries)
    bounds = jnp.cumsum(doc_lengths[0])[:-1]
    half = rows_here // 2
    starts = jnp.stack([ctx_place * rows_here, (ctx_size - 1 - ctx_place) * rows_here + half])
    place = jnp.concatenate([bounds, starts]).astype(jnp.int32)
    attn_out, queries_wide = attend(place, queries, kv_all)
    attended = swap_halves(attn_out.astype(jnp.bfloat16))
    attn_partial = mat_product(attended, out_full)
    residual = (
        tokens_f + lax.psum(attn_partial.astype(jnp.bfloat16), "tp").astype(jnp.float32) + out_shift
    )
    normed_two = layer_norm(residual, gain_two, shift_two).astype(jnp.bfloat16)
    hidden = mat_product(normed_two, in_full) + in_shift
    active, gelu_pull = jax.vjp(smooth_act, hidden)
    active = active.astype(jnp.bfloat16)
    grad_active = right_product(cotangent, back_full)
    grad_hidden = gelu_pull(grad_active)[0].astype(jnp.bfloat16)
    norm_two_partial = right_product(grad_hidden, in_full)
    grad_normed_two = lax.psum(norm_two_partial.astype(jnp.bfloat16), "tp").astype(jnp.float32)
    ff_partial = mat_product(active, back_full)
    mixed = (
        residual + lax.psum(ff_partial.astype(jnp.bfloat16), "tp").astype(jnp.float32) + back_shift
    ).astype(jnp.bfloat16)
    back_shift_grad = column_sums(cotangent)
    back_grad = left_product(cotangent, active).astype(jnp.bfloat16)
    in_shift_grad = column_sums(grad_hidden)
    in_grad = left_product(normed_two, grad_hidden).astype(jnp.bfloat16)
    ff_width = in_grad.shape[1]
    ff_sum = reduce_shards(
        jnp.concatenate(
            [
                in_grad.reshape(fsdp, part_d, ff_width),
                back_grad.reshape(fsdp, part_d, ff_width),
            ],
            axis=1,
        )
    )
    unused, second_pull = jax.vjp(layer_norm, residual, gain_two, shift_two)
    grad_residual, gain_two_grad, shift_two_grad = second_pull(grad_normed_two)
    grad_residual = cot_f + grad_residual
    grad_attn = grad_residual.astype(jnp.bfloat16)
    out_shift_grad = column_sums(grad_attn)
    grad_attended = right_product(grad_attn, out_full).astype(jnp.bfloat16)
    out_grad = left_product(grad_attn, attended).astype(jnp.bfloat16)
    grad_swapped = swap_halves(grad_attended)
    grad_queries, kv_terms = attend_back(place, queries_wide, grad_swapped, attn_out, kv_all)
    grad_queries = swap_halves(grad_queries)
    grad_kv = lax.psum_scatter(kv_terms, "ctx", scatter_dimension=0, tiled=True)
    grad_keys = grad_kv[:, :local_width]
    grad_values = grad_kv[:, local_width:]
    norm_one_partial = (
        right_product(grad_queries, qkv_full[0])
        + right_product(grad_keys, qkv_full[1])
        + right_product(grad_values, qkv_full[2])
    )
    grad_normed_one = lax.psum(norm_one_partial.astype(jnp.bfloat16), "tp").astype(jnp.float32)
    unused, first_pull = jax.vjp(layer_norm, tokens_f, gain_one, shift_one)
    grad_tokens, gain_one_grad, shift_one_grad = first_pull(grad_normed_one)
    input_rows = grad_residual + grad_tokens
    head_parts = [
        part.astype(jnp.bfloat16).reshape(fsdp, part_d, local_width)
        for part in (
            left_product(normed_one, grad_queries),
            left_product(normed_one, grad_keys),
            left_product(normed_one, grad_values),
            out_grad,
        )
    ]
    head_sum = reduce_shards(jnp.concatenate(head_parts, axis=1))
    vector_parts = [
        part.reshape(fsdp, -1)
        for part in (
            gain_one_grad,
            shift_one_grad,
            gain_two_grad,
            shift_two_grad,
            out_shift_grad,
            back_shift_grad,
            column_sums(grad_queries),
            column_sums(grad_values),
            in_shift_grad,
        )
    ]
    vector_sum = jnp.concatenate(vector_parts, axis=1).reshape(-1)
    vector_sum = lax.psum(vector_sum, ("fsdp", "ctx")).reshape(fsdp, -1)
    vector_sum = lax.dynamic_index_in_dim(vector_sum, lax.axis_index("fsdp"), 0, keepdims=False)
    vector_out, offset = [], 0
    for size in sizes:
        vector_out.append(vector_sum[offset : offset + size])
        offset += size
    head_sum = head_sum.astype(jnp.float32)
    qkv_sum = head_sum[: 3 * part_d].reshape(3, part_d, local_width)
    out_sum = head_sum[3 * part_d :].T
    ff_sum = ff_sum.astype(jnp.float32)
    return (
        mixed,
        input_rows,
        vector_out[0],
        vector_out[1],
        vector_out[2],
        vector_out[3],
        qkv_sum,
        jnp.stack([vector_out[6], vector_out[7]]),
        out_sum,
        vector_out[4],
        ff_sum[:part_d],
        vector_out[8],
        ff_sum[part_d:].T,
        vector_out[5],
    )


def solution(mesh):
    return jax.shard_map(
        on_device,
        mesh=mesh,
        in_specs=(
            P(("fsdp", "ctx"), None),
            P(("fsdp", "ctx"), None),
            P("fsdp", None),
            P("fsdp"),
            P("fsdp"),
            P("fsdp"),
            P("fsdp"),
            P(None, "fsdp", "tp"),
            P(None, ("tp", "fsdp")),
            P("tp", "fsdp"),
            P("fsdp"),
            P("fsdp", "tp"),
            P(("tp", "fsdp")),
            P("tp", "fsdp"),
            P("fsdp"),
        ),
        out_specs=(
            P(("fsdp", "ctx"), None),
            P(("fsdp", "ctx"), None),
            P("fsdp"),
            P("fsdp"),
            P("fsdp"),
            P("fsdp"),
            P(None, "fsdp", "tp"),
            P(None, ("tp", "fsdp")),
            P("tp", "fsdp"),
            P("fsdp"),
            P("fsdp", "tp"),
            P(("tp", "fsdp")),
            P("tp", "fsdp"),
            P("fsdp"),
        ),
        check_vma=False,
    )
```

```python
import jax
import jax.numpy as jnp
from jax import lax
from jax.experimental import pallas as pl
from jax.experimental.pallas import tpu as pltpu
from jax.sharding import PartitionSpec as P

HEAD = 64


norm_epsilon = 1e-05
masked_score = -1e30


def layer_norm(inputs_f, norm_gain, norm_shift):
    centred = inputs_f - jnp.mean(inputs_f, axis=-1, keepdims=True)
    spread = jnp.mean(centred * centred, axis=-1, keepdims=True)
    return centred * lax.rsqrt(spread + norm_epsilon) * norm_gain + norm_shift


def smooth_act(inputs_f):
    return jax.nn.gelu(inputs_f, approximate=True)


def mat_product(left_side, right_side):
    return jnp.dot(left_side, right_side, preferred_element_type=jnp.float32)


def left_product(left_side, right_side):
    return lax.dot_general(
        left_side, right_side, (((0,), (0,)), ((), ())), preferred_element_type=jnp.float32
    )


def right_product(left_side, right_side):
    return lax.dot_general(
        left_side, right_side, (((1,), (1,)), ((), ())), preferred_element_type=jnp.float32
    )


def column_sums(matrix):
    return jnp.sum(matrix.astype(jnp.float32), axis=0)


LANES = 128
Q_BLOCK = 256
K_BLOCK = 512
VMEM_BYTES = 60 * 1024 * 1024


def doc_start(place, bound_one, bound_two):
    return jnp.where(place >= bound_two, bound_two, jnp.where(place >= bound_one, bound_one, 0))


def widen(piece, tail):
    return jnp.concatenate([piece, tail], axis=1)


def lay_out_heads(kv_ref, key_s, value_s):
    heads, rows_all, _ = key_s.shape
    width = heads * HEAD
    lane = lax.broadcasted_iota(jnp.int32, (K_BLOCK, LANES - HEAD), 1)
    ones = jnp.where(lane < 3, 1.0, 0.0).astype(jnp.bfloat16)

    def step(block, carry):
        rows = pl.ds(pl.multiple_of(block * K_BLOCK, K_BLOCK), K_BLOCK)
        slab = kv_ref[rows, :]
        for h in range(heads):
            key_s[h, rows, :] = widen(slab[:, h * HEAD : (h + 1) * HEAD], ones)
            value_s[h, rows, :] = widen(slab[:, width + h * HEAD : width + (h + 1) * HEAD], ones)
        return carry

    lax.fori_loop(0, rows_all // K_BLOCK, step, 0)


def block_ranges(first, place_ref):
    bound_one, bound_two = place_ref[0], place_ref[1]
    last = first + Q_BLOCK - 1
    begin = doc_start(first, bound_one, bound_two) // K_BLOCK
    end = last // K_BLOCK + 1
    clear_from = (doc_start(last, bound_one, bound_two) + K_BLOCK - 1) // K_BLOCK
    clear_from = jnp.minimum(jnp.maximum(clear_from, begin), end)
    clear_to = jnp.minimum(jnp.maximum((first + 1) // K_BLOCK, clear_from), end)
    return begin, clear_from, clear_to, end


def three_loops(ranges, visit, carry):
    begin, clear_from, clear_to, end = ranges
    carry = lax.fori_loop(begin, clear_from, lambda i, c: visit(i, c, True), carry)
    carry = lax.fori_loop(clear_from, clear_to, lambda i, c: visit(i, c, False), carry)
    return lax.fori_loop(clear_to, end, lambda i, c: visit(i, c, True), carry)


def attend_kernel(place_ref, q_ref, kv_ref, out_ref, qa_ref, key_s, value_s, acc_s):
    heads = key_s.shape[0]
    lay_out_heads(kv_ref, key_s, value_s)
    half = q_ref.shape[0] // 2
    bound_one, bound_two = place_ref[0], place_ref[1]
    lane = lax.broadcasted_iota(jnp.int32, (Q_BLOCK, LANES), 1)
    zeros = jnp.zeros((Q_BLOCK, LANES - HEAD), jnp.float32)

    for part in range(2):

        def q_step(block, carry0, part=part):
            first = place_ref[2 + part] + block * Q_BLOCK
            rows = pl.ds(pl.multiple_of(part * half + block * Q_BLOCK, Q_BLOCK), Q_BLOCK)
            q_all = q_ref[rows, :].astype(jnp.float32) * (HEAD**-0.5)
            q_wide = [widen(q_all[:, h * HEAD : (h + 1) * HEAD], zeros) for h in range(heads)]
            q_low = [q.astype(jnp.bfloat16) for q in q_wide]
            acc_s[...] = jnp.zeros_like(acc_s)
            q_place = first + lax.broadcasted_iota(jnp.int32, (Q_BLOCK, 1), 0)
            q_start = doc_start(q_place, bound_one, bound_two)

            def visit(kb, maxima, masked):
                keys = pl.ds(pl.multiple_of(kb * K_BLOCK, K_BLOCK), K_BLOCK)
                if masked:
                    k_place = kb * K_BLOCK + lax.broadcasted_iota(
                        jnp.int32, (Q_BLOCK, K_BLOCK), 1
                    )
                    allowed = (k_place <= q_place) & (k_place >= q_start)
                new_maxima = []
                for h in range(heads):
                    scores = right_product(q_low[h], key_s[h, keys, :])
                    if masked:
                        scores = jnp.where(allowed, scores, masked_score)
                    new_max = jnp.maximum(maxima[h], jnp.max(scores, axis=1, keepdims=True))
                    prob = jnp.exp(scores - new_max).astype(jnp.bfloat16)
                    acc_s[h] = acc_s[h] * jnp.exp(maxima[h] - new_max) + mat_product(
                        prob, value_s[h, keys, :]
                    )
                    new_maxima.append(new_max)
                return tuple(new_maxima)

            start = tuple(jnp.full((Q_BLOCK, 1), masked_score, jnp.float32) for _ in range(heads))
            maxima = three_loops(block_ranges(first, place_ref), visit, start)
            outs = []
            for h in range(heads):
                total = acc_s[h]
                row_sum = total[:, HEAD : HEAD + 1]
                outs.append(total[:, :HEAD] / row_sum)
                minus = -(maxima[h] + jnp.log(row_sum))
                high = minus.astype(jnp.bfloat16).astype(jnp.float32)
                middle = (minus - high).astype(jnp.bfloat16).astype(jnp.float32)
                wide = jnp.where(lane == HEAD, high, q_wide[h])
                wide = jnp.where(lane == HEAD + 1, middle, wide)
                wide = jnp.where(lane == HEAD + 2, minus - high - middle, wide)
                qa_ref[h, rows, :] = wide.astype(jnp.bfloat16)
            out_ref[rows, :] = jnp.concatenate(outs, axis=1)
            return carry0

        lax.fori_loop(0, half // Q_BLOCK, q_step, 0)


def attend_back_kernel(
    place_ref, qa_ref, go_ref, out_ref, kv_ref, dq_ref, dkv_ref, key_s, value_s, dk_s, dv_s, dq_s
):
    heads, rows_all, _ = key_s.shape
    lay_out_heads(kv_ref, key_s, value_s)
    dk_s[...] = jnp.zeros_like(dk_s)
    dv_s[...] = jnp.zeros_like(dv_s)
    half = go_ref.shape[0] // 2
    bound_one, bound_two = place_ref[0], place_ref[1]
    lane = lax.broadcasted_iota(jnp.int32, (Q_BLOCK, LANES), 1)
    zeros = jnp.zeros((Q_BLOCK, LANES - HEAD), jnp.float32)

    for part in range(2):

        def q_step(block, carry0, part=part):
            first = place_ref[2 + part] + block * Q_BLOCK
            rows = pl.ds(pl.multiple_of(part * half + block * Q_BLOCK, Q_BLOCK), Q_BLOCK)
            go_all = go_ref[rows, :].astype(jnp.float32)
            weighted = go_all * out_ref[rows, :]
            go_low, q_low = [], []
            for h in range(heads):
                cols = slice(h * HEAD, (h + 1) * HEAD)
                minus = -jnp.sum(weighted[:, cols], axis=1, keepdims=True)
                high = minus.astype(jnp.bfloat16).astype(jnp.float32)
                wide = widen(go_all[:, cols], zeros)
                wide = jnp.where(lane == HEAD, high, wide)
                wide = jnp.where(lane == HEAD + 1, minus - high, wide)
                go_low.append(wide.astype(jnp.bfloat16))
                q_low.append(qa_ref[h, rows, :])
            dq_s[...] = jnp.zeros_like(dq_s)
            q_place = first + lax.broadcasted_iota(jnp.int32, (1, Q_BLOCK), 1)
            q_start = doc_start(q_place, bound_one, bound_two)

            def visit(kb, carry, masked):
                keys = pl.ds(pl.multiple_of(kb * K_BLOCK, K_BLOCK), K_BLOCK)
                if masked:
                    k_place = kb * K_BLOCK + lax.broadcasted_iota(
                        jnp.int32, (K_BLOCK, Q_BLOCK), 0
                    )
                    allowed = (k_place <= q_place) & (k_place >= q_start)
                for h in range(heads):
                    key_block = key_s[h, keys, :]
                    scores = right_product(key_block, q_low[h])
                    if masked:
                        scores = jnp.where(allowed, scores, masked_score)
                    prob = jnp.exp(scores)
                    grad_prob = right_product(value_s[h, keys, :], go_low[h])
                    grad_scores = (prob * grad_prob).astype(jnp.bfloat16)
                    dv_s[h, keys, :] += mat_product(prob.astype(jnp.bfloat16), go_low[h])
                    dk_s[h, keys, :] += mat_product(grad_scores, q_low[h])
                    dq_s[h] += left_product(grad_scores, key_block)
                return carry

            three_loops(block_ranges(first, place_ref), visit, 0)
            dq_ref[rows, :] = jnp.concatenate(
                [dq_s[h][:, :HEAD] * (HEAD**-0.5) for h in range(heads)], axis=1
            ).astype(jnp.bfloat16)
            return carry0

        lax.fori_loop(0, half // Q_BLOCK, q_step, 0)

    def store(block, carry):
        rows = pl.ds(pl.multiple_of(block * K_BLOCK, K_BLOCK), K_BLOCK)
        dkv_ref[rows, :] = jnp.concatenate(
            [dk_s[h, rows, :][:, :HEAD] for h in range(heads)]
            + [dv_s[h, rows, :][:, :HEAD] for h in range(heads)],
            axis=1,
        ).astype(jnp.bfloat16)
        return carry

    lax.fori_loop(0, rows_all // K_BLOCK, store, 0)


def in_vmem(count):
    return [pl.BlockSpec(memory_space=pltpu.VMEM)] * count


LINE_STEPS = 12


def line_sum_kernel(x_ref, out_ref, land, cross, part, send_e, recv_e, send_c, recv_c):
    me = lax.axis_index("tp")
    edge_peer = me + 1 - 2 * (me % 2)
    cross_peer = 3 - me
    inner = (me == 1) | (me == 2)
    step = x_ref.shape[0] // LINE_STEPS
    barrier = pltpu.get_barrier_semaphore()
    mesh_id = pl.DeviceIdType.MESH
    pl.semaphore_signal(barrier, inc=1, device_id={"tp": edge_peer}, device_id_type=mesh_id)

    @pl.when(inner)
    def _():
        pl.semaphore_signal(barrier, inc=1, device_id={"tp": cross_peer}, device_id_type=mesh_id)
        pl.semaphore_wait(barrier, 2)

    @pl.when(jnp.logical_not(inner))
    def _():
        pl.semaphore_wait(barrier, 1)

    def rows_of(c):
        return pl.ds(pl.multiple_of(c * step, step), step)

    def edge_copy(c, source):
        return pltpu.make_async_remote_copy(
            src_ref=source.at[rows_of(c)],
            dst_ref=land.at[rows_of(c)],
            send_sem=send_e.at[c],
            recv_sem=recv_e.at[c],
            device_id={"tp": edge_peer},
            device_id_type=mesh_id,
        )

    def cross_copy(c):
        return pltpu.make_async_remote_copy(
            src_ref=part.at[rows_of(c)],
            dst_ref=cross.at[rows_of(c)],
            send_sem=send_c.at[c],
            recv_sem=recv_c.at[c],
            device_id={"tp": cross_peer},
            device_id_type=mesh_id,
        )

    def add(left, right, c):
        total = left[rows_of(c), :].astype(jnp.float32) + right[rows_of(c), :].astype(jnp.float32)
        return total.astype(jnp.bfloat16)

    @pl.when(jnp.logical_not(inner))
    def _():
        @pl.loop(0, LINE_STEPS)
        def _(c):
            edge_copy(c, x_ref).start()

        @pl.loop(0, LINE_STEPS)
        def _(c):
            edge_copy(c, x_ref).wait_recv()
            out_ref[rows_of(c), :] = land[rows_of(c), :]

        @pl.loop(0, LINE_STEPS)
        def _(c):
            edge_copy(c, x_ref).wait_send()

    @pl.when(inner)
    def _():
        def first_half(c):
            edge_copy(c, out_ref).wait_recv()
            part[rows_of(c), :] = add(x_ref, land, c)
            cross_copy(c).start()

        def second_half(c):
            cross_copy(c).wait_recv()
            out_ref[rows_of(c), :] = add(part, cross, c)
            edge_copy(c, out_ref).start()

        first_half(0)

        @pl.loop(1, LINE_STEPS)
        def _(c):
            first_half(c)
            second_half(c - 1)

        second_half(LINE_STEPS - 1)

        @pl.loop(0, LINE_STEPS)
        def _(c):
            cross_copy(c).wait_send()
            edge_copy(c, out_ref).wait_send()


def line_sum(value, call):
    if lax.axis_size("tp") != 4 or value.shape[0] % (16 * LINE_STEPS) != 0:
        return lax.psum(value, "tp")
    buffer = pltpu.VMEM(value.shape, value.dtype)
    sems = pltpu.SemaphoreType.DMA((LINE_STEPS,))
    return pl.pallas_call(
        line_sum_kernel,
        out_shape=jax.ShapeDtypeStruct(value.shape, value.dtype),
        in_specs=in_vmem(1),
        out_specs=in_vmem(1)[0],
        scratch_shapes=[buffer, buffer, buffer, sems, sems, sems, sems],
        compiler_params=pltpu.CompilerParams(
            vmem_limit_bytes=VMEM_BYTES // 2, collective_id=call, has_side_effects=True
        ),
        cost_estimate=pl.CostEstimate(
            flops=50_000_000_000, bytes_accessed=4 << 20, transcendentals=0
        ),
    )(value)


def attend(place, queries, kv_all):
    rows, width = queries.shape
    rows_all = kv_all.shape[0]
    heads = width // HEAD
    pairs = rows * rows_all * heads // 2
    return pl.pallas_call(
        attend_kernel,
        out_shape=(
            jax.ShapeDtypeStruct((rows, width), jnp.float32),
            jax.ShapeDtypeStruct((heads, rows, LANES), jnp.bfloat16),
        ),
        in_specs=[pl.BlockSpec(memory_space=pltpu.SMEM)] + in_vmem(2),
        out_specs=tuple(in_vmem(2)),
        scratch_shapes=[
            pltpu.VMEM((heads, rows_all, LANES), jnp.bfloat16),
            pltpu.VMEM((heads, rows_all, LANES), jnp.bfloat16),
            pltpu.VMEM((heads, Q_BLOCK, LANES), jnp.float32),
        ],
        compiler_params=pltpu.CompilerParams(vmem_limit_bytes=VMEM_BYTES),
        cost_estimate=pl.CostEstimate(
            flops=pairs * 4 * 4 * HEAD, bytes_accessed=8 << 20, transcendentals=pairs
        ),
    )(place, queries, kv_all)


def attend_back(place, queries_wide, grad_out, attn_out, kv_all):
    rows, width = grad_out.shape
    rows_all = kv_all.shape[0]
    heads = width // HEAD
    pairs = rows * rows_all * heads // 2
    return pl.pallas_call(
        attend_back_kernel,
        out_shape=(
            jax.ShapeDtypeStruct((rows, width), jnp.bfloat16),
            jax.ShapeDtypeStruct((rows_all, 2 * width), jnp.bfloat16),
        ),
        in_specs=[pl.BlockSpec(memory_space=pltpu.SMEM)] + in_vmem(4),
        out_specs=tuple(in_vmem(2)),
        scratch_shapes=[
            pltpu.VMEM((heads, rows_all, LANES), jnp.bfloat16),
            pltpu.VMEM((heads, rows_all, LANES), jnp.bfloat16),
            pltpu.VMEM((heads, rows_all, LANES), jnp.float32),
            pltpu.VMEM((heads, rows_all, LANES), jnp.float32),
            pltpu.VMEM((heads, Q_BLOCK, LANES), jnp.float32),
        ],
        compiler_params=pltpu.CompilerParams(vmem_limit_bytes=VMEM_BYTES),
        cost_estimate=pl.CostEstimate(
            flops=pairs * 10 * 4 * HEAD, bytes_accessed=12 << 20, transcendentals=pairs
        ),
    )(place, queries_wide, grad_out, attn_out, kv_all)


def swap_halves(rows):
    size = lax.axis_size("ctx")
    half = rows.shape[0] // 2
    moved = lax.ppermute(rows[half:], "ctx", [(i, size - 1 - i) for i in range(size)])
    return jnp.concatenate([rows[:half], moved], axis=0)


def partner(value, distance):
    size = lax.axis_size("ctx")
    return lax.ppermute(value, "ctx", [(i, i ^ distance) for i in range(size)])


def halve(block, distance):
    bit = (lax.axis_index("ctx") // distance) % 2
    split = block.reshape(block.shape[:-2] + (2, block.shape[-2] // 2, block.shape[-1]))
    axis = split.ndim - 3
    keep = lax.dynamic_index_in_dim(split, bit, axis, keepdims=False)
    send = lax.dynamic_index_in_dim(split, 1 - bit, axis, keepdims=False)
    got = partner(send, distance)
    return (keep.astype(jnp.float32) + got.astype(jnp.float32)).astype(jnp.bfloat16)


def unhalve(block, distance):
    bit = (lax.axis_index("ctx") // distance) % 2
    other = partner(block, distance)
    low = jnp.where(bit == 0, block, other)
    high = jnp.where(bit == 0, other, block)
    return jnp.concatenate([low, high], axis=-2)


def sum_shards(vector):
    size = lax.axis_size("ctx")
    for i in range(size.bit_length() - 1):
        vector = vector + partner(vector, 1 << i)
    if lax.axis_size("fsdp") == 2:
        return vector + lax.ppermute(vector, "fsdp", [(0, 1), (1, 0)])
    return lax.psum(vector, "fsdp")


def reduce_shards(block):
    size = lax.axis_size("ctx")
    distances = [1 << i for i in range(size.bit_length() - 1)]
    block = halve(block, 1)
    if block.shape[0] == 2:
        bit = lax.axis_index("fsdp")
        keep = lax.dynamic_index_in_dim(block, bit, 0, keepdims=False)
        send = lax.dynamic_index_in_dim(block, 1 - bit, 0, keepdims=False)
        got = lax.ppermute(send, "fsdp", [(0, 1), (1, 0)])
        block = (keep.astype(jnp.float32) + got.astype(jnp.float32)).astype(jnp.bfloat16)
    else:
        block = lax.psum_scatter(block, "fsdp", scatter_dimension=0, tiled=False)
    for distance in distances[1:]:
        block = halve(block, distance)
    for distance in distances[::-1]:
        block = unhalve(block, distance)
    return block


def on_device(
    tokens,
    cotangent,
    doc_lengths,
    ln1_gain,
    ln1_bias,
    ln2_gain,
    ln2_bias,
    w_qkv,
    qv_bias,
    w_out,
    out_bias,
    w_in,
    in_bias,
    w_back,
    back_bias,
):
    rows_here = tokens.shape[0]
    ctx_size = lax.axis_size("ctx")
    ctx_place = lax.axis_index("ctx")
    fsdp = lax.axis_size("fsdp")
    model = tokens.shape[1]
    part_d = model // fsdp
    qkv_full = lax.all_gather(w_qkv, "fsdp", axis=1, tiled=True)
    vectors = jnp.concatenate(
        [
            ln1_gain,
            ln1_bias,
            ln2_gain,
            ln2_bias,
            out_bias,
            back_bias,
            qv_bias[0],
            qv_bias[1],
            in_bias,
        ]
    )
    vectors = lax.all_gather(vectors, "fsdp", axis=0).astype(jnp.float32)
    sizes = [part_d] * 6 + [qv_bias.shape[1]] * 2 + [in_bias.shape[0]]
    pieces, offset = [], 0
    for size in sizes:
        pieces.append(vectors[:, offset : offset + size].reshape(fsdp * size))
        offset += size
    gain_one, shift_one, gain_two, shift_two, out_shift, back_shift, q_shift, v_shift, in_shift = (
        pieces
    )
    out_full = lax.all_gather(w_out, "fsdp", axis=1, tiled=True)
    in_full = lax.all_gather(w_in, "fsdp", axis=0, tiled=True)
    back_full = lax.all_gather(w_back, "fsdp", axis=1, tiled=True)
    local_width = qkv_full.shape[2]
    tokens_f = tokens.astype(jnp.float32)
    cot_f = cotangent.astype(jnp.float32)
    normed_one = layer_norm(tokens_f, gain_one, shift_one).astype(jnp.bfloat16)
    key_rows = mat_product(normed_one, qkv_full[1]).astype(jnp.bfloat16)
    value_rows = (mat_product(normed_one, qkv_full[2]) + v_shift).astype(jnp.bfloat16)
    kv_all = lax.all_gather(
        jnp.concatenate([key_rows, value_rows], axis=1), "ctx", axis=0, tiled=True
    )
    queries = (mat_product(normed_one, qkv_full[0]) + q_shift).astype(jnp.bfloat16)
    queries = swap_halves(queries)
    bounds = jnp.cumsum(doc_lengths[0])[:-1]
    half = rows_here // 2
    starts = jnp.stack([ctx_place * rows_here, (ctx_size - 1 - ctx_place) * rows_here + half])
    place = jnp.concatenate([bounds, starts]).astype(jnp.int32)
    attn_out, queries_wide = attend(place, queries, kv_all)
    attended = swap_halves(attn_out.astype(jnp.bfloat16))
    attn_partial = mat_product(attended, out_full)
    residual = (
        tokens_f + line_sum(attn_partial.astype(jnp.bfloat16), 0).astype(jnp.float32) + out_shift
    )
    normed_two = layer_norm(residual, gain_two, shift_two).astype(jnp.bfloat16)
    hidden = mat_product(normed_two, in_full) + in_shift
    active, gelu_pull = jax.vjp(smooth_act, hidden)
    active = active.astype(jnp.bfloat16)
    grad_active = right_product(cotangent, back_full)
    grad_hidden = gelu_pull(grad_active)[0].astype(jnp.bfloat16)
    norm_two_partial = right_product(grad_hidden, in_full)
    grad_normed_two = line_sum(norm_two_partial.astype(jnp.bfloat16), 1).astype(jnp.float32)
    ff_partial = mat_product(active, back_full)
    mixed = (
        residual + lax.psum(ff_partial.astype(jnp.bfloat16), "tp").astype(jnp.float32) + back_shift
    ).astype(jnp.bfloat16)
    back_shift_grad = column_sums(cotangent)
    back_grad = left_product(cotangent, active).astype(jnp.bfloat16)
    in_shift_grad = column_sums(grad_hidden)
    in_grad = left_product(normed_two, grad_hidden).astype(jnp.bfloat16)
    ff_width = in_grad.shape[1]
    ff_sum = reduce_shards(
        jnp.concatenate(
            [
                in_grad.reshape(fsdp, part_d, ff_width),
                back_grad.reshape(fsdp, part_d, ff_width),
            ],
            axis=1,
        )
    )
    unused, second_pull = jax.vjp(layer_norm, residual, gain_two, shift_two)
    grad_residual, gain_two_grad, shift_two_grad = second_pull(grad_normed_two)
    grad_residual = cot_f + grad_residual
    grad_attn = grad_residual.astype(jnp.bfloat16)
    out_shift_grad = column_sums(grad_attn)
    grad_attended = right_product(grad_attn, out_full).astype(jnp.bfloat16)
    out_grad = left_product(grad_attn, attended).astype(jnp.bfloat16)
    grad_swapped = swap_halves(grad_attended)
    grad_queries, kv_terms = attend_back(place, queries_wide, grad_swapped, attn_out, kv_all)
    grad_queries = swap_halves(grad_queries)
    grad_kv = lax.psum_scatter(kv_terms, "ctx", scatter_dimension=0, tiled=True)
    grad_keys = grad_kv[:, :local_width]
    grad_values = grad_kv[:, local_width:]
    norm_one_partial = (
        right_product(grad_queries, qkv_full[0])
        + right_product(grad_keys, qkv_full[1])
        + right_product(grad_values, qkv_full[2])
    )
    grad_normed_one = line_sum(norm_one_partial.astype(jnp.bfloat16), 2).astype(jnp.float32)
    unused, first_pull = jax.vjp(layer_norm, tokens_f, gain_one, shift_one)
    grad_tokens, gain_one_grad, shift_one_grad = first_pull(grad_normed_one)
    input_rows = grad_residual + grad_tokens
    head_parts = [
        part.astype(jnp.bfloat16).reshape(fsdp, part_d, local_width)
        for part in (
            left_product(normed_one, grad_queries),
            left_product(normed_one, grad_keys),
            left_product(normed_one, grad_values),
            out_grad,
        )
    ]
    head_sum = reduce_shards(jnp.concatenate(head_parts, axis=1))
    vector_parts = [
        part.reshape(fsdp, -1)
        for part in (
            gain_one_grad,
            shift_one_grad,
            gain_two_grad,
            shift_two_grad,
            out_shift_grad,
            back_shift_grad,
            column_sums(grad_queries),
            column_sums(grad_values),
            in_shift_grad,
        )
    ]
    vector_sum = jnp.concatenate(vector_parts, axis=1).reshape(-1)
    vector_sum = sum_shards(vector_sum).reshape(fsdp, -1)
    vector_sum = lax.dynamic_index_in_dim(vector_sum, lax.axis_index("fsdp"), 0, keepdims=False)
    vector_out, offset = [], 0
    for size in sizes:
        vector_out.append(vector_sum[offset : offset + size])
        offset += size
    head_sum = head_sum.astype(jnp.float32)
    qkv_sum = head_sum[: 3 * part_d].reshape(3, part_d, local_width)
    out_sum = head_sum[3 * part_d :].T
    ff_sum = ff_sum.astype(jnp.float32)
    return (
        mixed,
        input_rows,
        vector_out[0],
        vector_out[1],
        vector_out[2],
        vector_out[3],
        qkv_sum,
        jnp.stack([vector_out[6], vector_out[7]]),
        out_sum,
        vector_out[4],
        ff_sum[:part_d],
        vector_out[8],
        ff_sum[part_d:].T,
        vector_out[5],
    )


def solution(mesh):
    return jax.shard_map(
        on_device,
        mesh=mesh,
        in_specs=(
            P(("fsdp", "ctx"), None),
            P(("fsdp", "ctx"), None),
            P("fsdp", None),
            P("fsdp"),
            P("fsdp"),
            P("fsdp"),
            P("fsdp"),
            P(None, "fsdp", "tp"),
            P(None, ("tp", "fsdp")),
            P("tp", "fsdp"),
            P("fsdp"),
            P("fsdp", "tp"),
            P(("tp", "fsdp")),
            P("tp", "fsdp"),
            P("fsdp"),
        ),
        out_specs=(
            P(("fsdp", "ctx"), None),
            P(("fsdp", "ctx"), None),
            P("fsdp"),
            P("fsdp"),
            P("fsdp"),
            P("fsdp"),
            P(None, "fsdp", "tp"),
            P(None, ("tp", "fsdp")),
            P("tp", "fsdp"),
            P("fsdp"),
            P("fsdp", "tp"),
            P(("tp", "fsdp")),
            P("tp", "fsdp"),
            P("fsdp"),
        ),
        check_vma=False,
    )
```

```python
import jax
import jax.numpy as jnp
from jax import lax
from jax.experimental import pallas as pl
from jax.experimental.pallas import tpu as pltpu
from jax.sharding import PartitionSpec as P

HEAD = 64


norm_epsilon = 1e-05
masked_score = -1e30


def layer_norm(inputs_f, norm_gain, norm_shift):
    centred = inputs_f - jnp.mean(inputs_f, axis=-1, keepdims=True)
    spread = jnp.mean(centred * centred, axis=-1, keepdims=True)
    return centred * lax.rsqrt(spread + norm_epsilon) * norm_gain + norm_shift


def smooth_act(inputs_f):
    return jax.nn.gelu(inputs_f, approximate=True)


def mat_product(left_side, right_side):
    return jnp.dot(left_side, right_side, preferred_element_type=jnp.float32)


def left_product(left_side, right_side):
    return lax.dot_general(
        left_side, right_side, (((0,), (0,)), ((), ())), preferred_element_type=jnp.float32
    )


def right_product(left_side, right_side):
    return lax.dot_general(
        left_side, right_side, (((1,), (1,)), ((), ())), preferred_element_type=jnp.float32
    )


def column_sums(matrix):
    return jnp.sum(matrix.astype(jnp.float32), axis=0)


LANES = 128
Q_BLOCK = 256
K_BLOCK = 512
VMEM_BYTES = 60 * 1024 * 1024


def doc_start(place, bound_one, bound_two):
    return jnp.where(place >= bound_two, bound_two, jnp.where(place >= bound_one, bound_one, 0))


def widen(piece, tail):
    return jnp.concatenate([piece, tail], axis=1)


def lay_out_heads(kv_ref, key_s, value_s):
    heads, rows_all, _ = key_s.shape
    width = heads * HEAD
    lane = lax.broadcasted_iota(jnp.int32, (K_BLOCK, LANES - HEAD), 1)
    ones = jnp.where(lane < 3, 1.0, 0.0).astype(jnp.bfloat16)

    def step(block, carry):
        rows = pl.ds(pl.multiple_of(block * K_BLOCK, K_BLOCK), K_BLOCK)
        slab = kv_ref[rows, :]
        for h in range(heads):
            key_s[h, rows, :] = widen(slab[:, h * HEAD : (h + 1) * HEAD], ones)
            value_s[h, rows, :] = widen(slab[:, width + h * HEAD : width + (h + 1) * HEAD], ones)
        return carry

    lax.fori_loop(0, rows_all // K_BLOCK, step, 0)


def block_ranges(first, place_ref):
    bound_one, bound_two = place_ref[0], place_ref[1]
    last = first + Q_BLOCK - 1
    begin = doc_start(first, bound_one, bound_two) // K_BLOCK
    end = last // K_BLOCK + 1
    clear_from = (doc_start(last, bound_one, bound_two) + K_BLOCK - 1) // K_BLOCK
    clear_from = jnp.minimum(jnp.maximum(clear_from, begin), end)
    clear_to = jnp.minimum(jnp.maximum((first + 1) // K_BLOCK, clear_from), end)
    return begin, clear_from, clear_to, end


def three_loops(ranges, visit, carry):
    begin, clear_from, clear_to, end = ranges
    carry = lax.fori_loop(begin, clear_from, lambda i, c: visit(i, c, True), carry)
    carry = lax.fori_loop(clear_from, clear_to, lambda i, c: visit(i, c, False), carry)
    return lax.fori_loop(clear_to, end, lambda i, c: visit(i, c, True), carry)


def attend_kernel(place_ref, q_ref, kv_ref, out_ref, qa_ref, key_s, value_s, acc_s):
    heads = key_s.shape[0]
    lay_out_heads(kv_ref, key_s, value_s)
    half = q_ref.shape[0] // 2
    bound_one, bound_two = place_ref[0], place_ref[1]
    lane = lax.broadcasted_iota(jnp.int32, (Q_BLOCK, LANES), 1)
    zeros = jnp.zeros((Q_BLOCK, LANES - HEAD), jnp.float32)

    for part in range(2):

        def q_step(block, carry0, part=part):
            first = place_ref[2 + part] + block * Q_BLOCK
            rows = pl.ds(pl.multiple_of(part * half + block * Q_BLOCK, Q_BLOCK), Q_BLOCK)
            q_all = q_ref[rows, :].astype(jnp.float32) * (HEAD**-0.5)
            q_wide = [widen(q_all[:, h * HEAD : (h + 1) * HEAD], zeros) for h in range(heads)]
            q_low = [q.astype(jnp.bfloat16) for q in q_wide]
            acc_s[...] = jnp.zeros_like(acc_s)
            q_place = first + lax.broadcasted_iota(jnp.int32, (Q_BLOCK, 1), 0)
            q_start = doc_start(q_place, bound_one, bound_two)

            def visit(kb, maxima, masked):
                keys = pl.ds(pl.multiple_of(kb * K_BLOCK, K_BLOCK), K_BLOCK)
                if masked:
                    k_place = kb * K_BLOCK + lax.broadcasted_iota(
                        jnp.int32, (Q_BLOCK, K_BLOCK), 1
                    )
                    allowed = (k_place <= q_place) & (k_place >= q_start)
                new_maxima = []
                for h in range(heads):
                    scores = right_product(q_low[h], key_s[h, keys, :])
                    if masked:
                        scores = jnp.where(allowed, scores, masked_score)
                    new_max = jnp.maximum(maxima[h], jnp.max(scores, axis=1, keepdims=True))
                    prob = jnp.exp(scores - new_max).astype(jnp.bfloat16)
                    acc_s[h] = acc_s[h] * jnp.exp(maxima[h] - new_max) + mat_product(
                        prob, value_s[h, keys, :]
                    )
                    new_maxima.append(new_max)
                return tuple(new_maxima)

            start = tuple(jnp.full((Q_BLOCK, 1), masked_score, jnp.float32) for _ in range(heads))
            maxima = three_loops(block_ranges(first, place_ref), visit, start)
            outs = []
            for h in range(heads):
                total = acc_s[h]
                row_sum = total[:, HEAD : HEAD + 1]
                outs.append(total[:, :HEAD] / row_sum)
                minus = -(maxima[h] + jnp.log(row_sum))
                high = minus.astype(jnp.bfloat16).astype(jnp.float32)
                middle = (minus - high).astype(jnp.bfloat16).astype(jnp.float32)
                wide = jnp.where(lane == HEAD, high, q_wide[h])
                wide = jnp.where(lane == HEAD + 1, middle, wide)
                wide = jnp.where(lane == HEAD + 2, minus - high - middle, wide)
                qa_ref[h, rows, :] = wide.astype(jnp.bfloat16)
            out_ref[rows, :] = jnp.concatenate(outs, axis=1)
            return carry0

        lax.fori_loop(0, half // Q_BLOCK, q_step, 0)


def attend_back_kernel(
    place_ref, qa_ref, go_ref, out_ref, kv_ref, dq_ref, dkv_ref, key_s, value_s, dk_s, dv_s, dq_s
):
    heads, rows_all, _ = key_s.shape
    lay_out_heads(kv_ref, key_s, value_s)
    dk_s[...] = jnp.zeros_like(dk_s)
    dv_s[...] = jnp.zeros_like(dv_s)
    half = go_ref.shape[0] // 2
    bound_one, bound_two = place_ref[0], place_ref[1]
    lane = lax.broadcasted_iota(jnp.int32, (Q_BLOCK, LANES), 1)
    zeros = jnp.zeros((Q_BLOCK, LANES - HEAD), jnp.float32)

    for part in range(2):

        def q_step(block, carry0, part=part):
            first = place_ref[2 + part] + block * Q_BLOCK
            rows = pl.ds(pl.multiple_of(part * half + block * Q_BLOCK, Q_BLOCK), Q_BLOCK)
            go_all = go_ref[rows, :].astype(jnp.float32)
            weighted = go_all * out_ref[rows, :]
            go_low, q_low = [], []
            for h in range(heads):
                cols = slice(h * HEAD, (h + 1) * HEAD)
                minus = -jnp.sum(weighted[:, cols], axis=1, keepdims=True)
                high = minus.astype(jnp.bfloat16).astype(jnp.float32)
                wide = widen(go_all[:, cols], zeros)
                wide = jnp.where(lane == HEAD, high, wide)
                wide = jnp.where(lane == HEAD + 1, minus - high, wide)
                go_low.append(wide.astype(jnp.bfloat16))
                q_low.append(qa_ref[h, rows, :])
            dq_s[...] = jnp.zeros_like(dq_s)
            q_place = first + lax.broadcasted_iota(jnp.int32, (1, Q_BLOCK), 1)
            q_start = doc_start(q_place, bound_one, bound_two)

            def visit(kb, carry, masked):
                keys = pl.ds(pl.multiple_of(kb * K_BLOCK, K_BLOCK), K_BLOCK)
                if masked:
                    k_place = kb * K_BLOCK + lax.broadcasted_iota(
                        jnp.int32, (K_BLOCK, Q_BLOCK), 0
                    )
                    allowed = (k_place <= q_place) & (k_place >= q_start)
                for h in range(heads):
                    key_block = key_s[h, keys, :]
                    scores = right_product(key_block, q_low[h])
                    if masked:
                        scores = jnp.where(allowed, scores, masked_score)
                    prob = jnp.exp(scores)
                    grad_prob = right_product(value_s[h, keys, :], go_low[h])
                    grad_scores = (prob * grad_prob).astype(jnp.bfloat16)
                    dv_s[h, keys, :] += mat_product(prob.astype(jnp.bfloat16), go_low[h])
                    dk_s[h, keys, :] += mat_product(grad_scores, q_low[h])
                    dq_s[h] += left_product(grad_scores, key_block)
                return carry

            three_loops(block_ranges(first, place_ref), visit, 0)
            dq_ref[rows, :] = jnp.concatenate(
                [dq_s[h][:, :HEAD] * (HEAD**-0.5) for h in range(heads)], axis=1
            ).astype(jnp.bfloat16)
            return carry0

        lax.fori_loop(0, half // Q_BLOCK, q_step, 0)

    def store(block, carry):
        rows = pl.ds(pl.multiple_of(block * K_BLOCK, K_BLOCK), K_BLOCK)
        dkv_ref[rows, :] = jnp.concatenate(
            [dk_s[h, rows, :][:, :HEAD] for h in range(heads)]
            + [dv_s[h, rows, :][:, :HEAD] for h in range(heads)],
            axis=1,
        ).astype(jnp.bfloat16)
        return carry

    lax.fori_loop(0, rows_all // K_BLOCK, store, 0)


def in_vmem(count):
    return [pl.BlockSpec(memory_space=pltpu.VMEM)] * count


LINE_STEPS = 12


def line_sum_kernel(x_ref, after_ref, out_ref, land, cross, part, send_e, recv_e, send_c, recv_c):
    me = lax.axis_index("tp")
    edge_peer = me + 1 - 2 * (me % 2)
    cross_peer = 3 - me
    inner = (me == 1) | (me == 2)
    step = x_ref.shape[0] // LINE_STEPS
    barrier = pltpu.get_barrier_semaphore()
    mesh_id = pl.DeviceIdType.MESH
    pl.semaphore_signal(barrier, inc=1, device_id={"tp": edge_peer}, device_id_type=mesh_id)

    @pl.when(inner)
    def _():
        pl.semaphore_signal(barrier, inc=1, device_id={"tp": cross_peer}, device_id_type=mesh_id)
        pl.semaphore_wait(barrier, 2)

    @pl.when(jnp.logical_not(inner))
    def _():
        pl.semaphore_wait(barrier, 1)

    def rows_of(c):
        return pl.ds(pl.multiple_of(c * step, step), step)

    def edge_copy(c, source):
        return pltpu.make_async_remote_copy(
            src_ref=source.at[rows_of(c)],
            dst_ref=land.at[rows_of(c)],
            send_sem=send_e.at[c],
            recv_sem=recv_e.at[c],
            device_id={"tp": edge_peer},
            device_id_type=mesh_id,
        )

    def cross_copy(c):
        return pltpu.make_async_remote_copy(
            src_ref=part.at[rows_of(c)],
            dst_ref=cross.at[rows_of(c)],
            send_sem=send_c.at[c],
            recv_sem=recv_c.at[c],
            device_id={"tp": cross_peer},
            device_id_type=mesh_id,
        )

    def add(left, right, c):
        total = left[rows_of(c), :].astype(jnp.float32) + right[rows_of(c), :].astype(jnp.float32)
        return total.astype(jnp.bfloat16)

    @pl.when(jnp.logical_not(inner))
    def _():
        @pl.loop(0, LINE_STEPS)
        def _(c):
            edge_copy(c, x_ref).start()

        @pl.loop(0, LINE_STEPS)
        def _(c):
            edge_copy(c, x_ref).wait_recv()
            out_ref[rows_of(c), :] = land[rows_of(c), :]

        @pl.loop(0, LINE_STEPS)
        def _(c):
            edge_copy(c, x_ref).wait_send()

    @pl.when(inner)
    def _():
        def first_half(c):
            edge_copy(c, out_ref).wait_recv()
            part[rows_of(c), :] = add(x_ref, land, c)
            cross_copy(c).start()

        def second_half(c):
            cross_copy(c).wait_recv()
            out_ref[rows_of(c), :] = add(part, cross, c)
            edge_copy(c, out_ref).start()

        first_half(0)

        @pl.loop(1, LINE_STEPS)
        def _(c):
            first_half(c)
            second_half(c - 1)

        second_half(LINE_STEPS - 1)

        @pl.loop(0, LINE_STEPS)
        def _(c):
            cross_copy(c).wait_send()
            edge_copy(c, out_ref).wait_send()


def line_sum(value, call, after):
    if lax.axis_size("tp") != 4 or value.shape[0] % (16 * LINE_STEPS) != 0:
        return lax.psum(value, "tp")
    buffer = pltpu.VMEM(value.shape, value.dtype)
    sems = pltpu.SemaphoreType.DMA((LINE_STEPS,))
    return pl.pallas_call(
        line_sum_kernel,
        out_shape=jax.ShapeDtypeStruct(value.shape, value.dtype),
        in_specs=in_vmem(1) + [pl.BlockSpec(memory_space=pl.ANY)],
        out_specs=in_vmem(1)[0],
        scratch_shapes=[buffer, buffer, buffer, sems, sems, sems, sems],
        compiler_params=pltpu.CompilerParams(
            vmem_limit_bytes=VMEM_BYTES // 2, collective_id=call, has_side_effects=True
        ),
        cost_estimate=pl.CostEstimate(
            flops=50_000_000_000, bytes_accessed=4 << 20, transcendentals=0
        ),
    )(value, after)


def attend(place, queries, kv_all):
    rows, width = queries.shape
    rows_all = kv_all.shape[0]
    heads = width // HEAD
    pairs = rows * rows_all * heads // 2
    return pl.pallas_call(
        attend_kernel,
        out_shape=(
            jax.ShapeDtypeStruct((rows, width), jnp.float32),
            jax.ShapeDtypeStruct((heads, rows, LANES), jnp.bfloat16),
        ),
        in_specs=[pl.BlockSpec(memory_space=pltpu.SMEM)] + in_vmem(2),
        out_specs=tuple(in_vmem(2)),
        scratch_shapes=[
            pltpu.VMEM((heads, rows_all, LANES), jnp.bfloat16),
            pltpu.VMEM((heads, rows_all, LANES), jnp.bfloat16),
            pltpu.VMEM((heads, Q_BLOCK, LANES), jnp.float32),
        ],
        compiler_params=pltpu.CompilerParams(vmem_limit_bytes=VMEM_BYTES),
        cost_estimate=pl.CostEstimate(
            flops=pairs * 4 * 4 * HEAD, bytes_accessed=8 << 20, transcendentals=pairs
        ),
    )(place, queries, kv_all)


def attend_back(place, queries_wide, grad_out, attn_out, kv_all):
    rows, width = grad_out.shape
    rows_all = kv_all.shape[0]
    heads = width // HEAD
    pairs = rows * rows_all * heads // 2
    return pl.pallas_call(
        attend_back_kernel,
        out_shape=(
            jax.ShapeDtypeStruct((rows, width), jnp.bfloat16),
            jax.ShapeDtypeStruct((rows_all, 2 * width), jnp.bfloat16),
        ),
        in_specs=[pl.BlockSpec(memory_space=pltpu.SMEM)] + in_vmem(4),
        out_specs=tuple(in_vmem(2)),
        scratch_shapes=[
            pltpu.VMEM((heads, rows_all, LANES), jnp.bfloat16),
            pltpu.VMEM((heads, rows_all, LANES), jnp.bfloat16),
            pltpu.VMEM((heads, rows_all, LANES), jnp.float32),
            pltpu.VMEM((heads, rows_all, LANES), jnp.float32),
            pltpu.VMEM((heads, Q_BLOCK, LANES), jnp.float32),
        ],
        compiler_params=pltpu.CompilerParams(vmem_limit_bytes=VMEM_BYTES),
        cost_estimate=pl.CostEstimate(
            flops=pairs * 10 * 4 * HEAD, bytes_accessed=12 << 20, transcendentals=pairs
        ),
    )(place, queries_wide, grad_out, attn_out, kv_all)


def swap_halves(rows):
    size = lax.axis_size("ctx")
    half = rows.shape[0] // 2
    moved = lax.ppermute(rows[half:], "ctx", [(i, size - 1 - i) for i in range(size)])
    return jnp.concatenate([rows[:half], moved], axis=0)


def partner(value, distance):
    size = lax.axis_size("ctx")
    return lax.ppermute(value, "ctx", [(i, i ^ distance) for i in range(size)])


def halve(block, distance):
    bit = (lax.axis_index("ctx") // distance) % 2
    split = block.reshape(block.shape[:-2] + (2, block.shape[-2] // 2, block.shape[-1]))
    axis = split.ndim - 3
    keep = lax.dynamic_index_in_dim(split, bit, axis, keepdims=False)
    send = lax.dynamic_index_in_dim(split, 1 - bit, axis, keepdims=False)
    got = partner(send, distance)
    return (keep.astype(jnp.float32) + got.astype(jnp.float32)).astype(jnp.bfloat16)


def unhalve(block, distance):
    bit = (lax.axis_index("ctx") // distance) % 2
    other = partner(block, distance)
    low = jnp.where(bit == 0, block, other)
    high = jnp.where(bit == 0, other, block)
    return jnp.concatenate([low, high], axis=-2)


def sum_shards(vector):
    size = lax.axis_size("ctx")
    for i in range(size.bit_length() - 1):
        vector = vector + partner(vector, 1 << i)
    if lax.axis_size("fsdp") == 2:
        return vector + lax.ppermute(vector, "fsdp", [(0, 1), (1, 0)])
    return lax.psum(vector, "fsdp")


def scatter_blocks(terms, zero):
    size = lax.axis_size("ctx")
    rows, width = terms.shape[0] // size, terms.shape[1]
    block = terms.reshape(size, rows, width)
    for i in range(size.bit_length() - 1):
        bit = (lax.axis_index("ctx") // (1 << i)) % 2
        split = block.reshape(block.shape[0] // 2, 2, rows, width)
        keep = lax.dynamic_index_in_dim(split, bit, 1, keepdims=False)
        send = lax.dynamic_index_in_dim(split, 1 - bit, 1, keepdims=False)
        got = partner(send, 1 << i).astype(jnp.float32) + zero
        block = (keep.astype(jnp.float32) + got).astype(jnp.bfloat16)
    return block.reshape(rows, width)


def reduce_shards(block):
    size = lax.axis_size("ctx")
    distances = [1 << i for i in range(size.bit_length() - 1)]
    block = halve(block, 1)
    if block.shape[0] == 2:
        bit = lax.axis_index("fsdp")
        keep = lax.dynamic_index_in_dim(block, bit, 0, keepdims=False)
        send = lax.dynamic_index_in_dim(block, 1 - bit, 0, keepdims=False)
        got = lax.ppermute(send, "fsdp", [(0, 1), (1, 0)])
        block = (keep.astype(jnp.float32) + got.astype(jnp.float32)).astype(jnp.bfloat16)
    else:
        block = lax.psum_scatter(block, "fsdp", scatter_dimension=0, tiled=False)
    for distance in distances[1:]:
        block = halve(block, distance)
    for distance in distances[::-1]:
        block = unhalve(block, distance)
    return block


def on_device(
    tokens,
    cotangent,
    doc_lengths,
    ln1_gain,
    ln1_bias,
    ln2_gain,
    ln2_bias,
    w_qkv,
    qv_bias,
    w_out,
    out_bias,
    w_in,
    in_bias,
    w_back,
    back_bias,
):
    rows_here = tokens.shape[0]
    ctx_size = lax.axis_size("ctx")
    ctx_place = lax.axis_index("ctx")
    fsdp = lax.axis_size("fsdp")
    model = tokens.shape[1]
    part_d = model // fsdp
    qkv_full = lax.all_gather(w_qkv, "fsdp", axis=1, tiled=True)
    vectors = jnp.concatenate(
        [
            ln1_gain,
            ln1_bias,
            ln2_gain,
            ln2_bias,
            out_bias,
            back_bias,
            qv_bias[0],
            qv_bias[1],
            in_bias,
        ]
    )
    vectors = lax.all_gather(vectors, "fsdp", axis=0).astype(jnp.float32)
    sizes = [part_d] * 6 + [qv_bias.shape[1]] * 2 + [in_bias.shape[0]]
    pieces, offset = [], 0
    for size in sizes:
        pieces.append(vectors[:, offset : offset + size].reshape(fsdp * size))
        offset += size
    gain_one, shift_one, gain_two, shift_two, out_shift, back_shift, q_shift, v_shift, in_shift = (
        pieces
    )
    out_full = lax.all_gather(w_out, "fsdp", axis=1, tiled=True)
    in_full = lax.all_gather(w_in, "fsdp", axis=0, tiled=True)
    back_full = lax.all_gather(w_back, "fsdp", axis=1, tiled=True)
    local_width = qkv_full.shape[2]
    tokens_f = tokens.astype(jnp.float32)
    cot_f = cotangent.astype(jnp.float32)
    normed_one = layer_norm(tokens_f, gain_one, shift_one).astype(jnp.bfloat16)
    key_rows = mat_product(normed_one, qkv_full[1]).astype(jnp.bfloat16)
    value_rows = (mat_product(normed_one, qkv_full[2]) + v_shift).astype(jnp.bfloat16)
    kv_all = lax.all_gather(
        jnp.concatenate([key_rows, value_rows], axis=1), "ctx", axis=0, tiled=True
    )
    queries = (mat_product(normed_one, qkv_full[0]) + q_shift).astype(jnp.bfloat16)
    queries = swap_halves(queries)
    bounds = jnp.cumsum(doc_lengths[0])[:-1]
    half = rows_here // 2
    starts = jnp.stack([ctx_place * rows_here, (ctx_size - 1 - ctx_place) * rows_here + half])
    place = jnp.concatenate([bounds, starts]).astype(jnp.int32)
    attn_out, queries_wide = attend(place, queries, kv_all)
    attended = swap_halves(attn_out.astype(jnp.bfloat16))
    attn_partial = mat_product(attended, out_full)
    residual = (
        tokens_f + line_sum(attn_partial.astype(jnp.bfloat16), 0, attended).astype(jnp.float32) + out_shift
    )
    normed_two = layer_norm(residual, gain_two, shift_two).astype(jnp.bfloat16)
    hidden = mat_product(normed_two, in_full) + in_shift
    active, gelu_pull = jax.vjp(smooth_act, hidden)
    active = active.astype(jnp.bfloat16)
    grad_active = right_product(cotangent, back_full)
    grad_hidden = gelu_pull(grad_active)[0].astype(jnp.bfloat16)
    norm_two_partial = right_product(grad_hidden, in_full)
    grad_normed_two = line_sum(norm_two_partial.astype(jnp.bfloat16), 1, active).astype(jnp.float32)
    grad_normed_two, active = lax.optimization_barrier((grad_normed_two, active))
    ff_partial = mat_product(active, back_full)
    ff_total = lax.psum(ff_partial.astype(jnp.bfloat16), "tp")
    back_shift_grad = column_sums(cotangent)
    back_grad = left_product(cotangent, active).astype(jnp.bfloat16)
    in_shift_grad = column_sums(grad_hidden)
    in_grad = left_product(normed_two, grad_hidden).astype(jnp.bfloat16)
    ff_width = in_grad.shape[1]
    ff_sum = reduce_shards(
        jnp.concatenate(
            [
                in_grad.reshape(fsdp, part_d, ff_width),
                back_grad.reshape(fsdp, part_d, ff_width),
            ],
            axis=1,
        )
    )
    unused, second_pull = jax.vjp(layer_norm, residual, gain_two, shift_two)
    grad_residual, gain_two_grad, shift_two_grad = second_pull(grad_normed_two)
    grad_residual = cot_f + grad_residual
    grad_attn = grad_residual.astype(jnp.bfloat16)
    out_shift_grad = column_sums(grad_attn)
    grad_attended = right_product(grad_attn, out_full).astype(jnp.bfloat16)
    out_grad = left_product(grad_attn, attended).astype(jnp.bfloat16)
    grad_swapped = swap_halves(grad_attended)
    grad_queries, kv_terms = attend_back(place, queries_wide, grad_swapped, attn_out, kv_all)
    residual_late, unused = lax.optimization_barrier((residual, grad_queries))
    mixed = (residual_late + ff_total.astype(jnp.float32) + back_shift).astype(jnp.bfloat16)
    grad_queries = swap_halves(grad_queries)
    grad_kv = scatter_blocks(kv_terms, ff_total[0, 0].astype(jnp.float32) * 0.0)
    grad_keys = grad_kv[:, :local_width]
    grad_values = grad_kv[:, local_width:]
    norm_one_partial = (
        right_product(grad_queries, qkv_full[0])
        + right_product(grad_keys, qkv_full[1])
        + right_product(grad_values, qkv_full[2])
    )
    grad_normed_one = line_sum(norm_one_partial.astype(jnp.bfloat16), 2, mixed).astype(jnp.float32)
    unused, first_pull = jax.vjp(layer_norm, tokens_f, gain_one, shift_one)
    grad_tokens, gain_one_grad, shift_one_grad = first_pull(grad_normed_one)
    input_rows = grad_residual + grad_tokens
    head_parts = [
        part.astype(jnp.bfloat16).reshape(fsdp, part_d, local_width)
        for part in (
            left_product(normed_one, grad_queries),
            left_product(normed_one, grad_keys),
            left_product(normed_one, grad_values),
            out_grad,
        )
    ]
    head_sum = reduce_shards(jnp.concatenate(head_parts, axis=1))
    vector_parts = [
        part.reshape(fsdp, -1)
        for part in (
            gain_one_grad,
            shift_one_grad,
            gain_two_grad,
            shift_two_grad,
            out_shift_grad,
            back_shift_grad,
            column_sums(grad_queries),
            column_sums(grad_values),
            in_shift_grad,
        )
    ]
    vector_sum = jnp.concatenate(vector_parts, axis=1).reshape(-1)
    vector_sum = sum_shards(vector_sum).reshape(fsdp, -1)
    vector_sum = lax.dynamic_index_in_dim(vector_sum, lax.axis_index("fsdp"), 0, keepdims=False)
    vector_out, offset = [], 0
    for size in sizes:
        vector_out.append(vector_sum[offset : offset + size])
        offset += size
    head_sum = head_sum.astype(jnp.float32)
    qkv_sum = head_sum[: 3 * part_d].reshape(3, part_d, local_width)
    out_sum = head_sum[3 * part_d :].T
    ff_sum = ff_sum.astype(jnp.float32)
    return (
        mixed,
        input_rows,
        vector_out[0],
        vector_out[1],
        vector_out[2],
        vector_out[3],
        qkv_sum,
        jnp.stack([vector_out[6], vector_out[7]]),
        out_sum,
        vector_out[4],
        ff_sum[:part_d],
        vector_out[8],
        ff_sum[part_d:].T,
        vector_out[5],
    )


def solution(mesh):
    return jax.shard_map(
        on_device,
        mesh=mesh,
        in_specs=(
            P(("fsdp", "ctx"), None),
            P(("fsdp", "ctx"), None),
            P("fsdp", None),
            P("fsdp"),
            P("fsdp"),
            P("fsdp"),
            P("fsdp"),
            P(None, "fsdp", "tp"),
            P(None, ("tp", "fsdp")),
            P("tp", "fsdp"),
            P("fsdp"),
            P("fsdp", "tp"),
            P(("tp", "fsdp")),
            P("tp", "fsdp"),
            P("fsdp"),
        ),
        out_specs=(
            P(("fsdp", "ctx"), None),
            P(("fsdp", "ctx"), None),
            P("fsdp"),
            P("fsdp"),
            P("fsdp"),
            P("fsdp"),
            P(None, "fsdp", "tp"),
            P(None, ("tp", "fsdp")),
            P("tp", "fsdp"),
            P("fsdp"),
            P("fsdp", "tp"),
            P(("tp", "fsdp")),
            P("tp", "fsdp"),
            P("fsdp"),
        ),
        check_vma=False,
    )
```
